256 devices in a mesh: chol: 8 (over z), vol: 32 (over y, x, core).
Axes of the slice: x: 4, y: 4, z: 8, core: 2. Of those that a mesh axis runs over, the one named last changes fastest.
Arguments:
- diag_block: float32 [1024, 1024], P('vol'), as said below
- rhs_diag: float32 [3, 1024], P(None, 'vol'), may hold values from -0.3125 to 0.3125
- panel_block: float32 [32768, 1024], P(('chol', 'vol')), may hold values from -0.625 to 0.625
- rhs_panel: float32 [3, 32768], P(None, ('chol', 'vol')), may hold values from -1.25 to 1.25
- trail: float32 [32768, 1024], P(('chol', 'vol')), may hold values from -6 to 6
- ctrl_xyz: float32 [3, 32768], P(None, ('chol', 'vol')), may hold values from 0 to 256, as said below
- node_xyz: float32 [3, 2097152], P(None, ('chol', 'vol')), may hold values from 0 to 256, as said below
- tile_blocks: int32 [16384, 8], P(('chol', 'vol')), may hold values from 0 to 255, as said below
- tile_count: int32 [16384], P(('chol', 'vol')), may hold values from 3 to 8, as said below
- face_area: float32 [3, 6, 2097152], P(None, None, ('chol', 'vol')), may hold values from -1.25 to 1.25
- edge_nbr: int32 [6, 2097152], P(None, ('chol', 'vol')), may hold values from 0 to 8447, as said below
- old_volume: float32 [2097152], P(('chol', 'vol')), may hold values from 0.5 to 2
Outputs:
- trail_out: float32 [32768, 1024], P(('chol', 'vol'))
- node_disp: float32 [3, 2097152], P(None, ('chol', 'vol'))
- new_volume: float32 [2097152], P(('chol', 'vol'))
The draws below stay inside these ranges and needn't reach their ends.
Inputs may be any that keep to these rules, and one draw needn't show every extreme that they name: diag_block is symmetric and each diagonal entry exceeds the sum of magnitudes of the other entries of its row by 0.05 or more. tile_count gives how many leading slots of a tile's list are used. `tile_blocks`: the used slots of a tile name consecutive control blocks in increasing order; the unused ones repeat its first block. `ctrl_xyz`: the first coordinate of control point j lies in [j // 128, j // 128 + 1). `node_xyz`: the first coordinate is a position along the hull in units of one control block's length. For node n at position p of its partition, edge_nbr[e, n] - p - 128 is a nonzero offset of at most 128 in magnitude.
All inputs are finite; a program needn't handle non-finite values.
Results may differ from the reference program's by a relative error of at most 0.0003.
Values sent between devices are 32-bit elements; how exact they have to be, the bound alone decides.
No kernel may reach another device: no remote copies, remote signals or barrier semaphores. Data moves between devices by JAX's collectives and lax.ppermute only.
A program may use at most 128 MiB of HBM per device.

```python
import jax
import jax.numpy as jnp
from jax import lax

NB = 1024
P_DEV = 128
TILE_DEV = 64
K = 8
E = 6
HALO = 128
ROWS = 32768
NCTRL = 32768
TRAIL_COLS = 1024
NCB = 256
NODE_DEV = 8192
NODES = 2097152
NTILES = 16384
N_CHOL = 8
N_VOL = 32
DEVICES = 256


reach_radius = 1.25


def draw_diag_block(key, part):
    dense_key, extra_key = jax.random.split(jax.random.fold_in(key, 3))
    row_ids = jnp.arange(NB, dtype=jnp.int32)
    spread = jax.random.uniform(dense_key, (NB, NB), jnp.float32, -1.0, 1.0)
    upper = row_ids[:, None] < row_ids[None, :]
    total = jnp.where(upper, spread, spread.T) * (0.2 / NB)
    for round_index in range(3):
        order_key, value_key, sign_key = jax.random.split(jax.random.fold_in(key, 100 + round_index), 3)
        order = jax.random.permutation(order_key, NB).astype(jnp.int32)
        place = jnp.argsort(order).astype(jnp.int32)
        mate_place = place + 1 - 2 * (place % 2)
        partner = order[mate_place]
        magnitude = jax.random.uniform(value_key, (NB // 2,), jnp.float32, 0.9, 1.0)
        sign_bits = jax.random.randint(sign_key, (NB // 2,), 0, 2)
        pair_value = jnp.where(sign_bits == 1, magnitude, -magnitude)
        value = pair_value[place // 2] * (0.8 / 3.0)
        total = total + jnp.where(row_ids[None, :] == partner[:, None], value[:, None], 0.0)
    extra = jax.random.uniform(extra_key, (NB,), jnp.float32, 0.05, 0.1)
    on_diag = row_ids[:, None] == row_ids[None, :]
    return jnp.where(on_diag, 1.0 + extra[:, None], total).astype(jnp.float32)


def tile_layout(key):
    layout_key = jax.random.fold_in(key, 7)
    level_key, jitter_key, place_key = jax.random.split(layout_key, 3)
    groups = NTILES // TILE_DEV
    extra_most = K - 3
    level = jnp.maximum(jax.random.randint(level_key, (groups,), 0, 2 * extra_most) - (extra_most - 1), 0)
    level = jnp.where(jnp.arange(groups, dtype=jnp.int32) == 0, extra_most, level)
    position = jnp.arange(NTILES, dtype=jnp.int32)
    own_level = level[position // TILE_DEV]
    jitter = jax.random.randint(jitter_key, (NTILES,), 0, 2)
    count = 3 + jnp.maximum(own_level - jitter, 0)
    count = jnp.where(position == 0, K, count)
    count = jnp.where(position == NTILES - 1, 3, count)
    spots = jax.random.randint(place_key, (NTILES,), 0, 1 << 20)
    first = spots % (NCB - count + 1)
    first = jnp.where(position == 0, 0, first)
    first = jnp.where(position == NTILES - 1, NCB - 3, first)
    return (first.astype(jnp.int32), count.astype(jnp.int32))


def draw_tile_blocks(key, part):
    first, count = tile_layout(key)
    slot_ids = jnp.arange(K, dtype=jnp.int32)
    offset = jnp.where(slot_ids[None, :] < count[:, None], slot_ids[None, :], 0)
    return (first[:, None] + offset).astype(jnp.int32)


def draw_tile_count(key, part):
    first, count = tile_layout(key)
    return count.astype(jnp.int32)


def draw_ctrl_xyz(key, part):
    unit = jax.random.uniform(jax.random.fold_in(key, 11), (3, NCTRL), jnp.float32, 0.0, 1.0)
    block_of = (jnp.arange(NCTRL, dtype=jnp.int32) // 128).astype(jnp.float32)
    along = block_of + unit[0]
    across = 0.5 * unit[1]
    height = unit[2]
    return jnp.stack([along, across, height]).astype(jnp.float32)


def draw_node_xyz(key, part):
    first, count = tile_layout(key)
    unit = jax.random.uniform(jax.random.fold_in(key, 13), (3, NODES), jnp.float32, 0.0, 1.0)
    tile_of = jnp.arange(NODES, dtype=jnp.int32) // 128
    low = first[tile_of].astype(jnp.float32)
    width = count[tile_of].astype(jnp.float32) - 2.0 * reach_radius
    along = low + reach_radius + unit[0] * width
    across = 0.25 + 0.5 * unit[1]
    height = unit[2]
    return jnp.stack([along, across, height]).astype(jnp.float32)


def draw_edge_nbr(key, part):
    key_size, key_sign = jax.random.split(key)
    step_size = jax.random.randint(key_size, (E, NODES), 1, HALO + 1)
    sign_bits = jax.random.randint(key_sign, (E, NODES), 0, 2)
    reach = jnp.where(sign_bits == 1, step_size, -step_size)
    local_pos = jnp.arange(NODES, dtype=jnp.int32) % NODE_DEV
    edge_row = jnp.arange(E, dtype=jnp.int32)[:, None]
    reach = jnp.where((edge_row == 0) & (local_pos[None, :] == 0), -HALO, reach)
    reach = jnp.where((edge_row == 0) & (local_pos[None, :] == NODE_DEV - 1), HALO, reach)
    return (local_pos[None, :] + HALO + reach).astype(jnp.int32)


def level_of(stream_key, shape, shards, smallest, high):
    def one(dim, blocks):
        heights = jax.random.uniform(jax.random.fold_in(jax.random.fold_in(stream_key, 6), dim), (blocks,), jnp.float32, smallest / len(shards), high / len(shards))
        return jnp.repeat(jnp.exp(heights), shape[dim] // blocks).reshape((-1,) + (1,) * (len(shape) - dim - 1))

    level = one(*shards[0])
    for cut in shards[1:]:
        level = level * one(*cut)
    return level


def bell_draw(rng, extent, scale, bound, cuts=(), held_as=jnp.bfloat16):
    entries = scale * jax.random.normal(rng, extent, jnp.float32)
    if cuts:
        entries = entries * level_of(rng, extent, cuts, -0.22, 0.18)
    return jnp.clip(entries, -bound, bound).astype(held_as)


def setup_inputs(seed: int = 0) -> dict:
    key_of = jax.random.split(jax.random.key(seed), 13)
    diag_block = draw_diag_block(jax.random.fold_in(key_of[12], 71), 0)
    rhs_diag = bell_draw(key_of[1], (3, NB), 0.05, 0.3125, ((1, 32),), jnp.float32)
    panel_block = bell_draw(key_of[2], (ROWS, NB), (3.5 * NB ** -0.5), 0.625, ((0, 256),), jnp.float32)
    rhs_panel = bell_draw(key_of[3], (3, NCTRL), 0.2, 1.25, ((1, 256),), jnp.float32)
    trail = bell_draw(key_of[4], (ROWS, TRAIL_COLS), 1.0, 6.0, ((0, 256),), jnp.float32)
    ctrl_xyz = draw_ctrl_xyz(jax.random.fold_in(key_of[12], 71), 0)
    node_xyz = draw_node_xyz(jax.random.fold_in(key_of[12], 71), 0)
    tile_blocks = draw_tile_blocks(jax.random.fold_in(key_of[12], 71), 0)
    tile_count = draw_tile_count(jax.random.fold_in(key_of[12], 71), 0)
    face_area = bell_draw(key_of[9], (3, E, NODES), 0.2, 1.25, ((2, 256),), jnp.float32)
    edge_nbr = draw_edge_nbr(jax.random.fold_in(key_of[12], 71), 0)
    old_volume = jnp.clip(0.5 + 1.5 * jax.random.uniform(key_of[11], (NODES,), jnp.float32) ** level_of(key_of[11], (NODES,), ((0, 256),), -0.2, 0.2), 0.5, 2.0)
    return dict(diag_block=diag_block, rhs_diag=rhs_diag, panel_block=panel_block, rhs_panel=rhs_panel, trail=trail, ctrl_xyz=ctrl_xyz, node_xyz=node_xyz, tile_blocks=tile_blocks, tile_count=tile_count, face_area=face_area, edge_nbr=edge_nbr, old_volume=old_volume)


highest_mode = lax.Precision.HIGHEST
support_radius = 1.25

def wendland(dist_sq):
    scaled = jnp.sqrt(dist_sq) / support_radius
    remain = jnp.maximum(1.0 - scaled, 0.0)
    return remain ** 4 * (4.0 * scaled + 1.0)

def slot_term(tile_xyz, chosen, live_mask, blocks_xyz, blocks_weight):
    near_xyz = blocks_xyz[:, chosen]
    near_weight = blocks_weight[:, chosen]
    dist_sq = jnp.zeros((tile_xyz.shape[1], 128, 128), jnp.float32)
    for axis_pos in range(3):
        differ = tile_xyz[axis_pos][:, :, None] - near_xyz[axis_pos][:, None, :]
        dist_sq = dist_sq + differ * differ
    kernel = wendland(dist_sq)
    term = jnp.einsum('tnc,atc->atn', kernel, near_weight, precision=highest_mode)
    return term * live_mask[None, :, None]

def reference(diag_block, rhs_diag, panel_block, rhs_panel, trail, ctrl_xyz, node_xyz, tile_blocks, tile_count, face_area, edge_nbr, old_volume):
    factor = jnp.linalg.cholesky(diag_block)
    lower_panel = jax.scipy.linalg.solve_triangular(factor, panel_block.T, lower=True).T
    forward = jax.scipy.linalg.solve_triangular(factor, rhs_diag.T, lower=True)
    ctrl_weight = rhs_panel - jnp.dot(lower_panel, forward, precision=highest_mode).T
    grouped = lower_panel.reshape(N_CHOL, N_VOL, P_DEV, NB)
    products = jnp.einsum('cvpk,dvqk->cvpdq', grouped, grouped, precision=highest_mode)
    trail_out = trail - products.reshape(ROWS, TRAIL_COLS)
    blocks_xyz = ctrl_xyz.reshape(3, NCB, 128)
    blocks_weight = ctrl_weight.reshape(3, NCB, 128)
    tiles_xyz = node_xyz.reshape(3, DEVICES, TILE_DEV, 128).transpose(1, 0, 2, 3)
    lists = tile_blocks.reshape(DEVICES, TILE_DEV, K)
    counts = tile_count.reshape(DEVICES, TILE_DEV)

    def device_tiles(inputs):
        tile_xyz, chosen_lists, count_row = inputs
        running = jnp.zeros((3, TILE_DEV, 128), jnp.float32)
        for slot_index in range(K):
            live_mask = (slot_index < count_row).astype(jnp.float32)
            running = running + slot_term(tile_xyz, chosen_lists[:, slot_index], live_mask, blocks_xyz, blocks_weight)
        return running
    per_device = lax.map(device_tiles, (tiles_xyz, lists, counts))
    node_disp = per_device.transpose(1, 0, 2, 3).reshape(3, NODES)
    strip_len = N_VOL * NODE_DEV
    strips = node_disp.reshape(3, N_CHOL, strip_len)
    padded = jnp.pad(strips, ((0, 0), (0, 0), (HALO, HALO)))
    node_ids = jnp.arange(NODES, dtype=jnp.int32)
    position = node_ids % strip_len
    base = position - position % NODE_DEV
    strip_of = node_ids // strip_len
    index = (base[None, :] + edge_nbr).astype(jnp.int32)
    across_disp = padded[:, strip_of[None, :], index]
    flux = lax.optimization_barrier(jnp.sum(face_area * (node_disp[:, None, :] + across_disp), axis=(0, 1)))
    new_volume = old_volume + 0.5 * flux
    return (trail_out, node_disp, new_volume)
```

```python
import jax
import jax.numpy as jnp
from jax import lax
from jax.experimental import pallas as pl
from jax.experimental.pallas import tpu as pltpu
from jax.sharding import PartitionSpec as P

F32 = jnp.float32
BF16 = jnp.bfloat16
NN = (((1,), (0,)), ((), ()))
NT = (((1,), (1,)), ((), ()))
WIDE = 256
STEPS = 4
ORDER = 1024
SIDE = 256
VMEM = pl.BlockSpec(memory_space=pltpu.VMEM)


def split(value):
    high = value.astype(BF16)
    return high, (value - high.astype(F32)).astype(BF16)


def raw_dot(left, right, dims=NN):
    return lax.dot_general(left, right, dims, preferred_element_type=F32)


def product(left, right, dims=NN):
    left_high, left_low = left
    right_high, right_low = right
    return (
        raw_dot(left_high, right_low, dims) + raw_dot(left_low, right_high, dims)
    ) + raw_dot(left_high, right_high, dims)


def inverse(block):
    size = block.shape[0]
    row_id = lax.broadcasted_iota(jnp.int32, (size, size), 0)
    col_id = lax.broadcasted_iota(jnp.int32, (size, size), 1)
    on_diag = row_id == col_id
    only_diag = jnp.where(on_diag, block, 0.0)
    diag_col = jnp.sum(only_diag, axis=1, keepdims=True)
    diag_row = jnp.sum(only_diag, axis=0, keepdims=True)
    power = jnp.where(on_diag, 0.0, -block / diag_col)
    total = jnp.where(on_diag, 1.0, power)
    parts = split(power)
    power = product(parts, parts)

    def stage(power, total):
        parts = split(power)
        return product(parts, parts), total + product(split(total), parts)

    for _ in range(4):
        power, total = stage(power, total)
    total = total + product(split(total), split(power))

    def left_over(power):
        return size * jnp.max(jnp.abs(power)) ** 2

    def unfinished(state):
        return (state[2] > 1e-7) & (state[3] < 40)

    def more(state):
        power, total, _, count = state
        parts = split(power)
        power = product(parts, parts)
        total = total + product(split(total), split(power))
        return power, total, left_over(power), count + 1

    total = lax.while_loop(unfinished, more, (power, total, left_over(power), 0))[1]
    return total / diag_row


def factor_body(rows_ref, panel_ref, out_ref, m_ref, vh_ref, vl_ref):
    full = ORDER + SIDE
    half_row = lax.broadcasted_iota(jnp.int32, (128, 128), 0) // 64
    half_col = lax.broadcasted_iota(jnp.int32, (128, 128), 1) // 64
    lane = lax.broadcasted_iota(jnp.int32, (128, 128), 1)
    def rows_of(g, m):
        return rows_ref[128 * g : 128 * g + 128, 128 * m : 128 * m + 128]
    for g in range(8):
        for h in range(g, 8):
            m = h - g
            if m < 4:
                block = rows_of(g, m)
            elif m == 4:
                block = jnp.where(half_row == half_col, rows_of(g, 4), rows_of(h, 4).T)
            else:
                block = rows_of(h, 8 - m).T
            m_ref[128 * g : 128 * g + 128, 128 * h : 128 * h + 128] = block
            if m == 1 and g % 2 == 0:
                m_ref[128 * h : 128 * h + 128, 128 * g : 128 * g + 128] = block.T
        m_ref[128 * g : 128 * g + 128, ORDER : ORDER + 128] = panel_ref[:, 128 * g : 128 * g + 128].T
        spare = rows_of(g, 4)
        turned = pltpu.roll(spare, 64, axis=1)
        first_half = (half_row == 1) if g < 4 else (half_row == 0)
        right = jnp.where(first_half, spare, turned)
        m_ref[128 * g : 128 * g + 128, ORDER + 128 : full] = jnp.where((lane >= 3) & (lane < 6), right, 0.0)
    for k in range(STEPS):
        here = slice(WIDE * k, WIDE * (k + 1))
        later = WIDE * (k + 1)
        inv = split(inverse(m_ref[here, here]))
        values = product(inv, split(m_ref[here, later:full]))
        if k < STEPS - 1:
            high, low = split(values)
            vh_ref[here, later:full] = high
            vl_ref[here, later:full] = low
            for i in range(k + 1, STEPS):
                there = slice(WIDE * i, WIDE * (i + 1))
                left = split(m_ref[here, there].T)
                start = WIDE * (i - k - 1)
                m_ref[there, WIDE * i : full] -= product(left, (high[:, start:], low[:, start:]))
        else:
            out_ref[here, :] = values
    for k in range(STEPS - 2, -1, -1):
        here = slice(WIDE * k, WIDE * (k + 1))
        later = WIDE * (k + 1)
        own = vh_ref[here, ORDER:full].astype(F32) + vl_ref[here, ORDER:full].astype(F32)
        left = (vh_ref[here, later:ORDER], vl_ref[here, later:ORDER])
        out_ref[here, :] = own - product(left, split(out_ref[later:ORDER, :]))


def solve_system(rows, panel):
    full = ORDER + SIDE
    return pl.pallas_call(
        factor_body,
        out_shape=jax.ShapeDtypeStruct((ORDER, SIDE), F32),
        in_specs=[VMEM, VMEM],
        out_specs=VMEM,
        scratch_shapes=[
            pltpu.VMEM((ORDER, full), F32),
            pltpu.VMEM((ORDER, full), BF16),
            pltpu.VMEM((ORDER, full), BF16),
        ],
        compiler_params=pltpu.CompilerParams(vmem_limit_bytes=56 * 2**20),
        name="block_elimination",
    )(rows, panel)


SLOTS = 8
TILES = 64
RADIUS = 1.25
PHI_SCALE = 4.0 * 0.8**5
UNROLL = 2


def products_body(x_ref, rows_ref, trail_ref, out_ref, ctrl_ref):
    x_parts = split(x_ref[...])
    for c in range(8):
        here = slice(128 * c, 128 * c + 128)
        both = product(split(rows_ref[c, 0:128, :]), x_parts)
        out_ref[:, here] = trail_ref[:, here] - both[:, 0:128].T
        ctrl_ref[c] = rows_ref[c, 128:136, 0:128] - both[:, 128:256].T[0:8]


def apply_products(x, rows, trail):
    return pl.pallas_call(
        products_body,
        out_shape=(
            jax.ShapeDtypeStruct((128, 1024), F32),
            jax.ShapeDtypeStruct((8, 8, 128), F32),
        ),
        in_specs=[VMEM] * 3,
        out_specs=(VMEM, VMEM),
        compiler_params=pltpu.CompilerParams(vmem_limit_bytes=56 * 2**20),
        name="trail_and_weights",
    )(x, rows, trail)


def tile_sum(t, first_ref, count_ref, nodes_ref, ctrl_ref):
    here = pl.ds(pl.multiple_of(t * 128, 128), 128)
    first = first_ref[t]
    count = count_ref[t]
    spread = [
        jnp.broadcast_to(nodes_ref[a : a + 1, here], (128, 128)).T for a in range(3)
    ]
    highs, lows, weights = [], [], []
    for s in range(SLOTS):
        live = s < count
        block = jnp.where(live, first + s, first)
        ctrl = ctrl_ref[block % 32, block // 32]
        dist_sq = jnp.zeros((128, 128), F32)
        for a in range(3):
            differ = spread[a] - ctrl[a : a + 1, :]
            dist_sq = dist_sq + differ * differ
        dist = dist_sq * lax.rsqrt(jnp.maximum(dist_sq, 1e-30))
        remain = jnp.maximum(RADIUS - dist, 0.0)
        remain_sq = remain * remain
        phi = remain_sq * remain_sq * (RADIUS * RADIUS - remain)
        high, low = split(phi)
        highs.append(high)
        lows.append(low)
        w_high, w_low = split(jnp.where(live, ctrl, 0.0))
        weights.append(jnp.concatenate([w_high, w_low], axis=0))
    weight = jnp.concatenate(weights, axis=1)
    by_high = raw_dot(weight, jnp.concatenate(highs, axis=1), NT)
    by_low = raw_dot(weight, jnp.concatenate(lows, axis=1), NT)
    return (by_low[0:8] + by_high[8:16] + by_high[0:8]) * PHI_SCALE


def mesh_body(first_ref, count_ref, nodes_ref, ctrl_ref, area_ref, nbr_ref, old_ref, disp_ref, volume_ref, d_ref):
    def sums(i, carry):
        for u in range(UNROLL):
            t = i * UNROLL + u
            d_ref[t] = tile_sum(t, first_ref, count_ref, nodes_ref, ctrl_ref)
        return carry

    lax.fori_loop(0, (TILES + 2) // UNROLL, sums, 0)

    def fluxes(i, carry):
        for u in range(2):
            t = i * 2 + u
            here = pl.ds(pl.multiple_of(t * 128, 128), 128)
            index = nbr_ref[:, here] - t * 128
            which = index // 128
            lane = index - which * 128
            own = d_ref[t + 1]
            disp_ref[:, here] = own[3:6]
            low, high = d_ref[t], d_ref[t + 2]
            flux = jnp.zeros((6, 128), F32)
            for a in range(3):
                near = [
                    jnp.take_along_axis(
                        jnp.broadcast_to(v[3 + a : 4 + a], (6, 128)), lane, axis=1, mode="promise_in_bounds"
                    )
                    for v in (low, own, high)
                ]
                across = jnp.where(which == 0, near[0], jnp.where(which == 1, near[1], near[2]))
                flux = flux + area_ref[a, :, here] * (own[3 + a : 4 + a] + across)
            volume_ref[pl.ds(t, 1), :] = old_ref[pl.ds(t, 1), :] + 0.5 * jnp.sum(flux, axis=0, keepdims=True)
        return carry

    lax.fori_loop(0, TILES // 2, fluxes, 0)


def update_mesh(first, count, nodes, ctrl, area, nbr, old):
    SMEM = pl.BlockSpec(memory_space=pltpu.SMEM)
    return pl.pallas_call(
        mesh_body,
        out_shape=(
            jax.ShapeDtypeStruct((3, TILES * 128), F32),
            jax.ShapeDtypeStruct((TILES, 128), F32),
        ),
        in_specs=[SMEM, SMEM] + [VMEM] * 5,
        out_specs=(VMEM, VMEM),
        scratch_shapes=[pltpu.VMEM((TILES + 2, 8, 128), F32)],
        compiler_params=pltpu.CompilerParams(vmem_limit_bytes=56 * 2**20),
        name="rbf_and_flux",
    )(first, count, nodes, ctrl, area, nbr, old)


def pack_body(group_ref, diag_ref, rhs_diag_ref, panel_ref, xyz_ref, rhs_ref, rows_ref, send_ref):
    group = group_ref[0]
    part = group_ref[1]
    for m in range(5):
        column = lax.rem(group + m, 8) * 128
        rows_ref[:, 128 * m : 128 * m + 128] = diag_ref[:, pl.ds(pl.multiple_of(column, 128), 128)]
    tall = jnp.concatenate([jnp.zeros((3, 32), F32), rhs_diag_ref[...], jnp.zeros((2, 32), F32)], axis=0)
    wide = jnp.concatenate([tall, jnp.zeros((8, 96), F32)], axis=1)
    column = jnp.concatenate([wide, jnp.zeros((120, 128), F32)], axis=0).T[0:32]
    column = column + pltpu.roll(column, 64, axis=1)
    half = lax.broadcasted_iota(jnp.int32, (32, 128), 1) // 64
    kept = jnp.where(group < 4, part // 2, 1 - part // 2)
    rows_ref[:, 512:640] = jnp.where(half == kept, rows_ref[:, 512:640], column)
    send_ref[0:128, :] = panel_ref[...]
    send_ref[128:136, :] = jnp.zeros((8, 1024), F32)
    send_ref[128:131, 0:128] = xyz_ref[...]
    send_ref[131:134, 0:128] = rhs_ref[...]


def pack(place, diag, rhs_diag, panel, xyz, rhs):
    return pl.pallas_call(
        pack_body,
        out_shape=(jax.ShapeDtypeStruct((32, 640), F32), jax.ShapeDtypeStruct((136, 1024), F32)),
        in_specs=[pl.BlockSpec(memory_space=pltpu.SMEM)] + [VMEM] * 5,
        out_specs=(VMEM, VMEM),
        name="pack_rows",
    )(place, diag, rhs_diag, panel, xyz, rhs)


def to_all(block, axis):
    copies = jnp.broadcast_to(block[None], (lax.axis_size(axis),) + block.shape)
    return lax.all_to_all(copies, axis, 0, 0, tiled=True)


def per_device(
    diag_block,
    rhs_diag,
    panel_block,
    rhs_panel,
    trail,
    ctrl_xyz,
    node_xyz,
    tile_blocks,
    tile_count,
    face_area,
    edge_nbr,
    old_volume,
):
    place = lax.axis_index("vol")
    place = jnp.stack([place // 4, place % 4])
    rows, send = pack(place, diag_block, rhs_diag, panel_block, ctrl_xyz, rhs_panel)
    column_rows = lax.all_gather(send, "chol", axis=0, tiled=False)
    whole_rows = to_all(rows, "vol").reshape(1024, 640)

    def edge(tile):
        lists = jnp.stack([tile_blocks[tile, 0], tile_count[tile]]).astype(F32)
        xyz = node_xyz[:, -128:] if tile else node_xyz[:, :128]
        return jnp.concatenate([xyz, jnp.pad(lists[None], ((0, 4), (0, 126)))], axis=0)

    count = lax.axis_size("vol")
    forward = [(i, i + 1) for i in range(count - 1)]
    backward = [(i + 1, i) for i in range(count - 1)]
    low = lax.ppermute(edge(-1), "vol", forward)
    high = lax.ppermute(edge(0), "vol", backward)
    nodes = jnp.concatenate([low[0:3], node_xyz, high[0:3]], axis=1)
    firsts = jnp.concatenate([low[3, 0:1].astype(jnp.int32), tile_blocks[:, 0], high[3, 0:1].astype(jnp.int32)])
    counts = jnp.concatenate([low[3, 1:2].astype(jnp.int32), tile_count, high[3, 1:2].astype(jnp.int32)])

    x = solve_system(whole_rows, panel_block)
    trail_out, ctrl = apply_products(x, column_rows, trail)
    ctrl = to_all(ctrl, "vol")
    node_disp, new_volume = update_mesh(
        firsts, counts, nodes, ctrl, face_area, edge_nbr, old_volume.reshape(TILES, 128)
    )
    return (trail_out, node_disp, new_volume.reshape(-1))


def solution(mesh):
    return jax.shard_map(
        per_device,
        mesh=mesh,
        in_specs=(
            P("vol", None),
            P(None, "vol"),
            P(("chol", "vol"), None),
            P(None, ("chol", "vol")),
            P(("chol", "vol"), None),
            P(None, ("chol", "vol")),
            P(None, ("chol", "vol")),
            P(("chol", "vol"), None),
            P(("chol", "vol")),
            P(None, None, ("chol", "vol")),
            P(None, ("chol", "vol")),
            P(("chol", "vol")),
        ),
        out_specs=(P(("chol", "vol"), None), P(None, ("chol", "vol")), P(("chol", "vol"))),
        check_vma=False,
    )
```

```python
import jax
import jax.numpy as jnp
from jax import lax
from jax.experimental import pallas as pl
from jax.experimental.pallas import tpu as pltpu
from jax.sharding import PartitionSpec as P

F32 = jnp.float32
BF16 = jnp.bfloat16
NN = (((1,), (0,)), ((), ()))
NT = (((1,), (1,)), ((), ()))
WIDE = 256
STEPS = 4
CHIPS = 16
ORDER = 1024
SIDE = 256
VMEM = pl.BlockSpec(memory_space=pltpu.VMEM)
SMEM = pl.BlockSpec(memory_space=pltpu.SMEM)


def split(value):
    high = value.astype(BF16)
    return high, (value - high.astype(F32)).astype(BF16)


def raw_dot(left, right, dims=NN):
    return lax.dot_general(left, right, dims, preferred_element_type=F32)


def product(left, right, dims=NN):
    left_high, left_low = left
    right_high, right_low = right
    return (
        raw_dot(left_high, right_low, dims) + raw_dot(left_low, right_high, dims)
    ) + raw_dot(left_high, right_high, dims)


def inverse(block):
    size = block.shape[0]
    row_id = lax.broadcasted_iota(jnp.int32, (size, size), 0)
    col_id = lax.broadcasted_iota(jnp.int32, (size, size), 1)
    on_diag = row_id == col_id
    only_diag = jnp.where(on_diag, block, 0.0)
    diag_col = jnp.sum(only_diag, axis=1, keepdims=True)
    diag_row = jnp.sum(only_diag, axis=0, keepdims=True)
    power = jnp.where(on_diag, 0.0, -block / diag_col)
    total = jnp.where(on_diag, 1.0, power)
    parts = split(power)
    power = product(parts, parts)

    def stage(power, total):
        parts = split(power)
        return product(parts, parts), total + product(split(total), parts)

    for _ in range(4):
        power, total = stage(power, total)
    total = total + product(split(total), split(power))

    def left_over(power):
        return size * jnp.max(jnp.abs(power)) ** 2

    def unfinished(state):
        return (state[2] > 1e-7) & (state[3] < 40)

    def more(state):
        power, total, _, count = state
        parts = split(power)
        power = product(parts, parts)
        total = total + product(split(total), split(power))
        return power, total, left_over(power), count + 1

    total = lax.while_loop(unfinished, more, (power, total, left_over(power), 0))[1]
    return total / diag_row


def factor_body(same_ref, other_ref, panel_ref, out_ref, rhs_ref, rows_ref, m_ref, vh_ref, vl_ref):
    full = ORDER + SIDE
    core = lax.axis_index("vol") % 2
    for i in range(16):
        rows_ref[pl.ds(pl.multiple_of(64 * i + 32 * core, 32), 32), :] = same_ref[i]
        rows_ref[pl.ds(pl.multiple_of(64 * i + 32 * (1 - core), 32), 32), :] = other_ref[i]
    half_row = lax.broadcasted_iota(jnp.int32, (128, 128), 0) // 64
    half_col = lax.broadcasted_iota(jnp.int32, (128, 128), 1) // 64
    lane = lax.broadcasted_iota(jnp.int32, (128, 128), 1)
    def rows_of(g, m):
        return rows_ref[128 * g : 128 * g + 128, 128 * m : 128 * m + 128]
    for g in range(8):
        for h in range(g, 8):
            m = h - g
            if m < 4:
                block = rows_of(g, m)
            elif m == 4:
                block = jnp.where(half_row == half_col, rows_of(g, 4), rows_of(h, 4).T)
            else:
                block = rows_of(h, 8 - m).T
            m_ref[128 * g : 128 * g + 128, 128 * h : 128 * h + 128] = block
            if m == 1 and g % 2 == 0:
                m_ref[128 * h : 128 * h + 128, 128 * g : 128 * g + 128] = block.T
        m_ref[128 * g : 128 * g + 128, ORDER : ORDER + 128] = panel_ref[:, 128 * g : 128 * g + 128].T
        spare = rows_of(g, 4)
        turned = pltpu.roll(spare, 64, axis=1)
        first_half = (half_row == 1) if g < 4 else (half_row == 0)
        right = jnp.where(first_half, spare, turned)
        m_ref[128 * g : 128 * g + 128, ORDER + 128 : full] = jnp.where((lane >= 3) & (lane < 6), right, 0.0)
    for k in range(STEPS):
        here = slice(WIDE * k, WIDE * (k + 1))
        later = WIDE * (k + 1)
        inv = split(inverse(m_ref[here, here]))
        values = product(inv, split(m_ref[here, later:full]))
        if k < STEPS - 1:
            high, low = split(values)
            vh_ref[here, later:full] = high
            vl_ref[here, later:full] = low
            for i in range(k + 1, STEPS):
                there = slice(WIDE * i, WIDE * (i + 1))
                left = split(m_ref[here, there].T)
                start = WIDE * (i - k - 1)
                m_ref[there, WIDE * i : full] -= product(left, (high[:, start:], low[:, start:]))
        else:
            out_ref[here, :] = values
    for k in range(STEPS - 2, -1, -1):
        here = slice(WIDE * k, WIDE * (k + 1))
        later = WIDE * (k + 1)
        own = vh_ref[here, ORDER:full].astype(F32) + vl_ref[here, ORDER:full].astype(F32)
        left = (vh_ref[here, later:ORDER], vl_ref[here, later:ORDER])
        out_ref[here, :] = own - product(left, split(out_ref[later:ORDER, :]))
    for g in range(8):
        here = slice(128 * g, 128 * g + 128)
        high, low = split(out_ref[here, 128:256].T[0:8])
        rhs_ref[:, here] = jnp.concatenate([high, low], axis=0)


def solve_system(same, other, panel):
    full = ORDER + SIDE
    return pl.pallas_call(
        factor_body,
        out_shape=(jax.ShapeDtypeStruct((ORDER, SIDE), F32), jax.ShapeDtypeStruct((16, ORDER), BF16)),
        in_specs=[VMEM] * 3,
        out_specs=(VMEM, VMEM),
        scratch_shapes=[
            pltpu.VMEM((ORDER, 640), F32),
            pltpu.VMEM((ORDER, full), F32),
            pltpu.VMEM((ORDER, full), BF16),
            pltpu.VMEM((ORDER, full), BF16),
        ],
        compiler_params=pltpu.CompilerParams(vmem_limit_bytes=56 * 2**20),
        name="block_elimination",
    )(same, other, panel)


SLOTS = 8
TILES = 64
RADIUS = 1.25
PHI_SCALE = 4.0 * 0.8**5
UNROLL = 6


def weights_body(rhs_ref, rows_ref, ctrl_ref):
    for c in range(2):
        high, low = split(rows_ref[c, 0:128, :])
        by_high = raw_dot(rhs_ref[...], high, NT)
        by_low = raw_dot(rhs_ref[...], low, NT)
        ctrl = rows_ref[c, 128:136, 0:128] - (by_low[0:8] + by_high[8:16] + by_high[0:8])
        ctrl_ref[:, c] = jnp.broadcast_to(ctrl, (CHIPS, 8, 128))


def control_weights(rhs, rows):
    return pl.pallas_call(
        weights_body,
        out_shape=jax.ShapeDtypeStruct((CHIPS, 8, 8, 128), F32),
        grid=(4,),
        in_specs=[
            pl.BlockSpec((16, ORDER), lambda c: (0, 0)),
            pl.BlockSpec((2, 136, ORDER), lambda c: (c, 0, 0)),
        ],
        out_specs=pl.BlockSpec((CHIPS, 2, 8, 128), lambda c: (0, c, 0, 0)),
        compiler_params=pltpu.CompilerParams(vmem_limit_bytes=60 * 2**20),
        name="control_weights",
    )(rhs, rows)


def products_body(x_ref, rows_ref, trail_ref, out_ref, high_ref, low_ref):
    @pl.when(pl.program_id(0) == 0)
    def _():
        high_ref[...], low_ref[...] = split(x_ref[...])

    sums = product(split(rows_ref[0, 0:128, :]), (high_ref[...], low_ref[...]))
    out_ref[...] = trail_ref[...] - sums.T


def apply_products(x, rows, trail):
    return pl.pallas_call(
        products_body,
        out_shape=jax.ShapeDtypeStruct((128, ORDER), F32),
        grid=(8,),
        in_specs=[
            pl.BlockSpec((ORDER, 128), lambda c: (0, 0)),
            pl.BlockSpec((1, 136, ORDER), lambda c: (c, 0, 0)),
            pl.BlockSpec((128, 128), lambda c: (0, c)),
        ],
        out_specs=pl.BlockSpec((128, 128), lambda c: (0, c)),
        scratch_shapes=[pltpu.VMEM((ORDER, 128), BF16)] * 2,
        compiler_params=pltpu.CompilerParams(vmem_limit_bytes=60 * 2**20),
        cost_estimate=pl.CostEstimate(flops=3 * 2 * 128 * 1024 * 1024, bytes_accessed=6 * 2**20, transcendentals=0),
        name="trail_update",
    )(x, rows, trail)


def tile_sum(t, first_ref, count_ref, nodes_ref, same_ref, other_ref):
    here = pl.ds(pl.multiple_of(t * 128, 128), 128)
    core = lax.axis_index("vol") % 2
    first = first_ref[t]
    count = count_ref[t]
    spread = [
        jnp.broadcast_to(nodes_ref[a : a + 1, here], (128, 128)).T for a in range(3)
    ]
    highs, lows, weights = [], [], []
    for s in range(SLOTS):
        live = s < count
        block = jnp.where(live, first + s, first)
        chip, rank = (block // 2) % CHIPS, block // 32
        ctrl = jnp.where(block % 2 == core, same_ref[chip, rank], other_ref[chip, rank])
        dist_sq = jnp.zeros((128, 128), F32)
        for a in range(3):
            differ = spread[a] - ctrl[a : a + 1, :]
            dist_sq = dist_sq + differ * differ
        dist = dist_sq * lax.rsqrt(jnp.maximum(dist_sq, 1e-30))
        remain = jnp.maximum(RADIUS - dist, 0.0)
        remain_sq = remain * remain
        phi = remain_sq * remain_sq * (RADIUS * RADIUS - remain)
        high, low = split(phi)
        highs.append(high)
        lows.append(low)
        w_high, w_low = split(jnp.where(live, ctrl, 0.0))
        weights.append(jnp.concatenate([w_high, w_low], axis=0))
    weight = jnp.concatenate(weights, axis=1)
    by_high = raw_dot(weight, jnp.concatenate(highs, axis=1), NT)
    by_low = raw_dot(weight, jnp.concatenate(lows, axis=1), NT)
    return (by_low[0:8] + by_high[8:16] + by_high[0:8]) * PHI_SCALE


def mesh_body(
    tile_first_ref,
    tile_count_ref,
    low_list_ref,
    high_list_ref,
    low_ref,
    high_ref,
    own_ref,
    same_ref,
    other_ref,
    area_ref,
    nbr_ref,
    old_ref,
    disp_ref,
    volume_ref,
    first_ref,
    count_ref,
    nodes_ref,
    d_ref,
):
    def lists(t, carry):
        first_ref[t + 1] = tile_first_ref[t]
        count_ref[t + 1] = tile_count_ref[t]
        return carry

    lax.fori_loop(0, TILES, lists, 0)
    for t, list_ref in ((0, low_list_ref), (TILES + 1, high_list_ref)):
        first_ref[t] = list_ref[3, 0].astype(jnp.int32)
        count_ref[t] = list_ref[3, 1].astype(jnp.int32)
    nodes_ref[:, 0:128] = low_ref[0:3]
    nodes_ref[:, 128 : 128 + TILES * 128] = own_ref[...]
    nodes_ref[:, 128 + TILES * 128 :] = high_ref[0:3]

    def sums(i, carry):
        for u in range(UNROLL):
            t = i * UNROLL + u
            d_ref[t] = tile_sum(t, first_ref, count_ref, nodes_ref, same_ref, other_ref)
        return carry

    lax.fori_loop(0, (TILES + 2) // UNROLL, sums, 0)

    def fluxes(i, carry):
        for u in range(4):
            t = i * 4 + u
            here = pl.ds(pl.multiple_of(t * 128, 128), 128)
            index = nbr_ref[:, here] - t * 128
            which = index // 128
            lane = index - which * 128
            own = d_ref[t + 1]
            disp_ref[:, here] = own[3:6]
            low, high = d_ref[t], d_ref[t + 2]
            flux = jnp.zeros((6, 128), F32)
            for a in range(3):
                near = [
                    jnp.take_along_axis(
                        jnp.broadcast_to(v[3 + a : 4 + a], (6, 128)), lane, axis=1, mode="promise_in_bounds"
                    )
                    for v in (low, own, high)
                ]
                across = jnp.where(which == 0, near[0], jnp.where(which == 1, near[1], near[2]))
                flux = flux + area_ref[a, :, here] * (own[3 + a : 4 + a] + across)
            volume_ref[pl.ds(t, 1), :] = old_ref[pl.ds(t, 1), :] + 0.5 * jnp.sum(flux, axis=0, keepdims=True)
        return carry

    lax.fori_loop(0, TILES // 4, fluxes, 0)


def update_mesh(first, count, low, high, nodes, same, other, area, nbr, old):
    return pl.pallas_call(
        mesh_body,
        out_shape=(
            jax.ShapeDtypeStruct((3, TILES * 128), F32),
            jax.ShapeDtypeStruct((TILES, 128), F32),
        ),
        in_specs=[SMEM] * 4 + [VMEM] * 8,
        out_specs=(VMEM, VMEM),
        scratch_shapes=[
            pltpu.SMEM((TILES + 2,), jnp.int32),
            pltpu.SMEM((TILES + 2,), jnp.int32),
            pltpu.VMEM((3, (TILES + 2) * 128), F32),
            pltpu.VMEM((TILES + 2, 8, 128), F32),
        ],
        compiler_params=pltpu.CompilerParams(vmem_limit_bytes=56 * 2**20),
        name="rbf_and_flux",
    )(first, count, low, high, low, high, nodes, same, other, area, nbr, old)


def send_body(panel_ref, xyz_ref, rhs_ref, send_ref):
    send_ref[0:128, :] = panel_ref[...]
    send_ref[128:136, :] = jnp.zeros((8, 1024), F32)
    send_ref[128:131, 0:128] = xyz_ref[...]
    send_ref[131:134, 0:128] = rhs_ref[...]


def pack_send(panel, xyz, rhs):
    return pl.pallas_call(
        send_body,
        out_shape=jax.ShapeDtypeStruct((136, ORDER), F32),
        in_specs=[VMEM] * 3,
        out_specs=VMEM,
        name="pack_panel",
    )(panel, xyz, rhs)


def pack_body(
    first_ref, count_ref, diag_ref, rhs_diag_ref, nodes_ref, rows_ref, head_ref, tail_ref
):
    place = lax.axis_index("vol")
    group, part = place // 4, place % 4
    for m in range(4):
        column = lax.rem(group + m, 8) * 128
        value = diag_ref[:, pl.ds(pl.multiple_of(column, 128), 128)]
        rows_ref[:, :, 128 * m : 128 * m + 128] = jnp.broadcast_to(value, (CHIPS, 32, 128))
    tall = jnp.concatenate([jnp.zeros((3, 32), F32), rhs_diag_ref[...], jnp.zeros((2, 32), F32)], axis=0)
    wide = jnp.concatenate([tall, jnp.zeros((8, 96), F32)], axis=1)
    column = jnp.concatenate([wide, jnp.zeros((120, 128), F32)], axis=0).T[0:32]
    column = column + pltpu.roll(column, 64, axis=1)
    half = lax.broadcasted_iota(jnp.int32, (32, 128), 1) // 64
    kept = jnp.where(group < 4, part // 2, 1 - part // 2)
    fifth = diag_ref[:, pl.ds(pl.multiple_of(lax.rem(group + 4, 8) * 128, 128), 128)]
    rows_ref[:, :, 512:640] = jnp.broadcast_to(jnp.where(half == kept, fifth, column), (CHIPS, 32, 128))
    row_id = lax.broadcasted_iota(jnp.int32, (8, 128), 0)
    lane = lax.broadcasted_iota(jnp.int32, (8, 128), 1)
    for edge_ref, tile in ((head_ref, 0), (tail_ref, TILES - 1)):
        first = first_ref[tile].astype(F32)
        count = count_ref[tile].astype(F32)
        lists = jnp.where(lane == 0, first, jnp.where(lane == 1, count, 0.0))
        edge_ref[...] = jnp.where(row_id == 3, lists, 0.0)
        edge_ref[0:3, :] = nodes_ref[:, 128 * tile : 128 * tile + 128]


def pack(first, count, diag, rhs_diag, nodes):
    edge = jax.ShapeDtypeStruct((8, 128), F32)
    return pl.pallas_call(
        pack_body,
        out_shape=(
            jax.ShapeDtypeStruct((CHIPS, 32, 640), F32),
            edge,
            edge,
        ),
        in_specs=[SMEM] * 2 + [VMEM] * 3,
        out_specs=(VMEM,) * 3,
        name="pack_rows",
    )(first, count, diag, rhs_diag, nodes)


def chips_to_all(copies):
    groups = [[2 * i + core for i in range(CHIPS)] for core in range(2)]
    return lax.all_to_all(copies, "vol", 0, 0, tiled=True, axis_index_groups=groups)


def other_core(blocks):
    return lax.ppermute(blocks, "vol", [(i, i ^ 1) for i in range(2 * CHIPS)])


def per_device(
    diag_block,
    rhs_diag,
    panel_block,
    rhs_panel,
    trail,
    ctrl_xyz,
    node_xyz,
    tile_blocks,
    tile_count,
    face_area,
    edge_nbr,
    old_volume,
):
    firsts = tile_blocks[:, 0]
    rows, head, tail = pack(firsts, tile_count, diag_block, rhs_diag, node_xyz)
    column_rows = lax.all_gather(pack_send(panel_block, ctrl_xyz, rhs_panel), "chol", axis=0, tiled=False)
    same_rows = chips_to_all(rows)
    other_rows = other_core(same_rows)
    size = lax.axis_size("vol")
    low = lax.ppermute(tail, "vol", [(i, i + 1) for i in range(size - 1)])
    high = lax.ppermute(head, "vol", [(i + 1, i) for i in range(size - 1)])
    other_rows, low, high = lax.optimization_barrier((other_rows, low, high))
    x, rhs_solved = solve_system(same_rows, other_rows, panel_block)
    same_ctrl = chips_to_all(control_weights(rhs_solved, column_rows))
    trail_out = apply_products(x, column_rows, trail)
    same_ctrl, trail_out = lax.optimization_barrier((same_ctrl, trail_out))
    other_ctrl = other_core(same_ctrl)
    node_disp, new_volume = update_mesh(
        firsts, tile_count, low, high, node_xyz, same_ctrl, other_ctrl, face_area, edge_nbr, old_volume.reshape(TILES, 128)
    )
    return (trail_out, node_disp, new_volume.reshape(-1))


def solution(mesh):
    return jax.shard_map(
        per_device,
        mesh=mesh,
        in_specs=(
            P("vol", None),
            P(None, "vol"),
            P(("chol", "vol"), None),
            P(None, ("chol", "vol")),
            P(("chol", "vol"), None),
            P(None, ("chol", "vol")),
            P(None, ("chol", "vol")),
            P(("chol", "vol"), None),
            P(("chol", "vol")),
            P(None, None, ("chol", "vol")),
            P(None, ("chol", "vol")),
            P(("chol", "vol")),
        ),
        out_specs=(P(("chol", "vol"), None), P(None, ("chol", "vol")), P(("chol", "vol"))),
        check_vma=False,
    )
```

```python
import jax
import jax.numpy as jnp
from jax import lax
from jax.experimental import pallas as pl
from jax.experimental.pallas import tpu as pltpu
from jax.sharding import PartitionSpec as P

F32 = jnp.float32
BF16 = jnp.bfloat16
NN = (((1,), (0,)), ((), ()))
NT = (((1,), (1,)), ((), ()))
WIDE = 256
STEPS = 4
CHIPS = 16
ORDER = 1024
SIDE = 256
VMEM = pl.BlockSpec(memory_space=pltpu.VMEM)
SMEM = pl.BlockSpec(memory_space=pltpu.SMEM)
ANY = pl.BlockSpec(memory_space=pl.ANY)


def split(value):
    high = value.astype(BF16)
    return high, (value - high.astype(F32)).astype(BF16)


def raw_dot(left, right, dims=NN):
    return lax.dot_general(left, right, dims, preferred_element_type=F32)


def product(left, right, dims=NN):
    left_high, left_low = left
    right_high, right_low = right
    return (
        raw_dot(left_high, right_low, dims) + raw_dot(left_low, right_high, dims)
    ) + raw_dot(left_high, right_high, dims)


def inverse(block):
    size = block.shape[0]
    row_id = lax.broadcasted_iota(jnp.int32, (size, size), 0)
    col_id = lax.broadcasted_iota(jnp.int32, (size, size), 1)
    on_diag = row_id == col_id
    only_diag = jnp.where(on_diag, block, 0.0)
    diag_col = jnp.sum(only_diag, axis=1, keepdims=True)
    diag_row = jnp.sum(only_diag, axis=0, keepdims=True)
    power = jnp.where(on_diag, 0.0, -block / diag_col)
    total = jnp.where(on_diag, 1.0, power)
    parts = split(power)
    power = product(parts, parts)

    def stage(power, total):
        parts = split(power)
        return product(parts, parts), total + product(split(total), parts)

    for _ in range(4):
        power, total = stage(power, total)
    total = total + product(split(total), split(power))

    def left_over(power):
        return size * jnp.max(jnp.abs(power)) ** 2

    def unfinished(state):
        return (state[2] > 1e-7) & (state[3] < 40)

    def more(state):
        power, total, _, count = state
        parts = split(power)
        power = product(parts, parts)
        total = total + product(split(total), split(power))
        return power, total, left_over(power), count + 1

    total = lax.while_loop(unfinished, more, (power, total, left_over(power), 0))[1]
    return total / diag_row


def factor_body(same_ref, other_ref, panel_ref, out_ref, rhs_ref, rows_ref, m_ref, vh_ref, vl_ref):
    full = ORDER + SIDE
    core = lax.axis_index("vol") % 2
    for i in range(16):
        rows_ref[pl.ds(pl.multiple_of(64 * i + 32 * core, 32), 32), :] = same_ref[i]
        rows_ref[pl.ds(pl.multiple_of(64 * i + 32 * (1 - core), 32), 32), :] = other_ref[i]
    half_row = lax.broadcasted_iota(jnp.int32, (128, 128), 0) // 64
    half_col = lax.broadcasted_iota(jnp.int32, (128, 128), 1) // 64
    lane = lax.broadcasted_iota(jnp.int32, (128, 128), 1)
    def rows_of(g, m):
        return rows_ref[128 * g : 128 * g + 128, 128 * m : 128 * m + 128]
    for g in range(8):
        for h in range(g, 8):
            m = h - g
            if m < 4:
                block = rows_of(g, m)
            elif m == 4:
                block = jnp.where(half_row == half_col, rows_of(g, 4), rows_of(h, 4).T)
            else:
                block = rows_of(h, 8 - m).T
            m_ref[128 * g : 128 * g + 128, 128 * h : 128 * h + 128] = block
            if m == 1 and g % 2 == 0:
                m_ref[128 * h : 128 * h + 128, 128 * g : 128 * g + 128] = block.T
        m_ref[128 * g : 128 * g + 128, ORDER : ORDER + 128] = panel_ref[:, 128 * g : 128 * g + 128].T
        spare = rows_of(g, 4)
        turned = pltpu.roll(spare, 64, axis=1)
        first_half = (half_row == 1) if g < 4 else (half_row == 0)
        right = jnp.where(first_half, spare, turned)
        m_ref[128 * g : 128 * g + 128, ORDER + 128 : full] = jnp.where((lane >= 3) & (lane < 6), right, 0.0)
    for k in range(STEPS):
        here = slice(WIDE * k, WIDE * (k + 1))
        later = WIDE * (k + 1)
        inv = split(inverse(m_ref[here, here]))
        values = product(inv, split(m_ref[here, later:full]))
        if k < STEPS - 1:
            high, low = split(values)
            vh_ref[here, later:full] = high
            vl_ref[here, later:full] = low
            for i in range(k + 1, STEPS):
                there = slice(WIDE * i, WIDE * (i + 1))
                left = split(m_ref[here, there].T)
                start = WIDE * (i - k - 1)
                m_ref[there, WIDE * i : full] -= product(left, (high[:, start:], low[:, start:]))
        else:
            out_ref[here, :] = values
    for k in range(STEPS - 2, -1, -1):
        here = slice(WIDE * k, WIDE * (k + 1))
        later = WIDE * (k + 1)
        own = vh_ref[here, ORDER:full].astype(F32) + vl_ref[here, ORDER:full].astype(F32)
        left = (vh_ref[here, later:ORDER], vl_ref[here, later:ORDER])
        out_ref[here, :] = own - product(left, split(out_ref[later:ORDER, :]))
    for g in range(8):
        here = slice(128 * g, 128 * g + 128)
        high, low = split(out_ref[here, 128:256].T[0:8])
        rhs_ref[:, here] = jnp.concatenate([high, low], axis=0)


def solve_system(same, other, panel):
    full = ORDER + SIDE
    return pl.pallas_call(
        factor_body,
        out_shape=(jax.ShapeDtypeStruct((ORDER, SIDE), F32), jax.ShapeDtypeStruct((16, ORDER), BF16)),
        in_specs=[VMEM] * 3,
        out_specs=(VMEM, VMEM),
        scratch_shapes=[
            pltpu.VMEM((ORDER, 640), F32),
            pltpu.VMEM((ORDER, full), F32),
            pltpu.VMEM((ORDER, full), BF16),
            pltpu.VMEM((ORDER, full), BF16),
        ],
        compiler_params=pltpu.CompilerParams(vmem_limit_bytes=56 * 2**20),
        name="block_elimination",
    )(same, other, panel)


SLOTS = 8
TILES = 64
RADIUS = 1.25
PHI_SCALE = 4.0 * 0.8**5
UNROLL = 11


def weights_body(rhs_ref, rows_ref, ctrl_ref):
    for c in range(4):
        high, low = split(rows_ref[c, 0:128, :])
        by_high = raw_dot(rhs_ref[...], high, NT)
        by_low = raw_dot(rhs_ref[...], low, NT)
        ctrl = rows_ref[c, 128:136, 0:128] - (by_low[0:8] + by_high[8:16] + by_high[0:8])
        ctrl_ref[:, c] = jnp.broadcast_to(ctrl, (CHIPS, 8, 128))


def control_weights(rhs, rows):
    return pl.pallas_call(
        weights_body,
        out_shape=jax.ShapeDtypeStruct((CHIPS, 8, 8, 128), F32),
        grid=(2,),
        in_specs=[
            pl.BlockSpec((16, ORDER), lambda c: (0, 0)),
            pl.BlockSpec((4, 136, ORDER), lambda c: (c, 0, 0)),
        ],
        out_specs=pl.BlockSpec((CHIPS, 4, 8, 128), lambda c: (0, c, 0, 0)),
        compiler_params=pltpu.CompilerParams(vmem_limit_bytes=60 * 2**20),
        name="control_weights",
    )(rhs, rows)


def products_body(x_ref, rows_ref, trail_ref, out_ref, high_ref, low_ref):
    @pl.when(pl.program_id(0) == 0)
    def _():
        high_ref[...], low_ref[...] = split(x_ref[...])

    sums = product(split(rows_ref[0, 0:128, :]), (high_ref[...], low_ref[...]))
    out_ref[...] = trail_ref[...] - sums.T


def apply_products(x, rows, trail):
    return pl.pallas_call(
        products_body,
        out_shape=jax.ShapeDtypeStruct((128, ORDER), F32),
        grid=(8,),
        in_specs=[
            pl.BlockSpec((ORDER, 128), lambda c: (0, 0)),
            pl.BlockSpec((1, 136, ORDER), lambda c: (c, 0, 0)),
            pl.BlockSpec((128, 128), lambda c: (0, c)),
        ],
        out_specs=pl.BlockSpec((128, 128), lambda c: (0, c)),
        scratch_shapes=[pltpu.VMEM((ORDER, 128), BF16)] * 2,
        compiler_params=pltpu.CompilerParams(vmem_limit_bytes=60 * 2**20),
        cost_estimate=pl.CostEstimate(flops=3 * 2 * 128 * 1024 * 1024, bytes_accessed=6 * 2**20, transcendentals=0),
        name="trail_update",
    )(x, rows, trail)


def tile_sum(t, first_ref, count_ref, nodes_ref, same_ref, other_ref):
    here = pl.ds(pl.multiple_of(t * 128, 128), 128)
    core = lax.axis_index("vol") % 2
    first = first_ref[t]
    count = count_ref[t]
    spread = [
        jnp.broadcast_to(nodes_ref[a : a + 1, here], (128, 128)).T for a in range(3)
    ]
    highs, lows, weights = [], [], []
    for s in range(SLOTS):
        live = s < count
        block = jnp.where(live, first + s, first)
        chip, rank = (block // 2) % CHIPS, block // 32
        ctrl = jnp.where(block % 2 == core, same_ref[chip, rank], other_ref[chip, rank])
        dist_sq = jnp.zeros((128, 128), F32)
        for a in range(3):
            differ = spread[a] - ctrl[a : a + 1, :]
            dist_sq = dist_sq + differ * differ
        dist = dist_sq * lax.rsqrt(jnp.maximum(dist_sq, 1e-30))
        remain = jnp.maximum(RADIUS - dist, 0.0)
        remain_sq = remain * remain
        phi = remain_sq * remain_sq * (RADIUS * RADIUS - remain)
        high, low = split(phi)
        highs.append(high)
        lows.append(low)
        w_high, w_low = split(jnp.where(live, ctrl, 0.0))
        weights.append(jnp.concatenate([w_high, w_low], axis=0))
    weight = jnp.concatenate(weights, axis=1)
    by_high = raw_dot(weight, jnp.concatenate(highs, axis=1), NT)
    by_low = raw_dot(weight, jnp.concatenate(lows, axis=1), NT)
    return (by_low[0:8] + by_high[8:16] + by_high[0:8]) * PHI_SCALE


def mesh_body(
    tile_first_ref,
    tile_count_ref,
    low_list_ref,
    high_list_ref,
    low_ref,
    high_ref,
    own_ref,
    same_any,
    other_any,
    area_ref,
    nbr_ref,
    old_ref,
    disp_ref,
    volume_ref,
    first_ref,
    count_ref,
    nodes_ref,
    d_ref,
    same_ref,
    other_ref,
    sems,
):
    copies = [
        pltpu.make_async_copy(same_any, same_ref, sems.at[0]),
        pltpu.make_async_copy(other_any, other_ref, sems.at[1]),
    ]
    for copy in copies:
        copy.start()

    def lists(t, carry):
        first_ref[t + 1] = tile_first_ref[t]
        count_ref[t + 1] = tile_count_ref[t]
        return carry

    lax.fori_loop(0, TILES, lists, 0)
    for t, list_ref in ((0, low_list_ref), (TILES + 1, high_list_ref)):
        first_ref[t] = list_ref[3, 0].astype(jnp.int32)
        count_ref[t] = list_ref[3, 1].astype(jnp.int32)
    nodes_ref[:, 0:128] = low_ref[0:3]
    nodes_ref[:, 128 : 128 + TILES * 128] = own_ref[...]
    nodes_ref[:, 128 + TILES * 128 :] = high_ref[0:3]

    def flux_tile(t):
        here = pl.ds(pl.multiple_of(t * 128, 128), 128)
        index = nbr_ref[:, here] - t * 128
        which = index // 128
        lane = index - which * 128
        low, own, high = d_ref[t], d_ref[t + 1], d_ref[t + 2]
        disp_ref[:, here] = own[3:6]
        flux = jnp.zeros((6, 128), F32)
        for a in range(3):
            near = [
                jnp.take_along_axis(
                    jnp.broadcast_to(v[3 + a : 4 + a], (6, 128)), lane, axis=1, mode="promise_in_bounds"
                )
                for v in (low, own, high)
            ]
            across = jnp.where(which == 0, near[0], jnp.where(which == 1, near[1], near[2]))
            flux = flux + area_ref[a, :, here] * (own[3 + a : 4 + a] + across)
        volume_ref[pl.ds(t, 1), :] = old_ref[pl.ds(t, 1), :] + 0.5 * jnp.sum(flux, axis=0, keepdims=True)

    def sums(i, carry):
        for u in range(UNROLL):
            flux_tile(jnp.maximum((i - 1) * UNROLL + u - 2, 0))
        for u in range(UNROLL):
            t = i * UNROLL + u
            d_ref[t] = tile_sum(t, first_ref, count_ref, nodes_ref, same_ref, other_ref)
        return carry

    d_ref[0:3] = jnp.zeros((3, 8, 128), F32)
    for copy in copies:
        copy.wait()
    lax.fori_loop(0, (TILES + 2) // UNROLL, sums, 0)
    for u in range(UNROLL):
        flux_tile(TILES - UNROLL + u)


def update_mesh(first, count, low, high, nodes, same, other, area, nbr, old):
    return pl.pallas_call(
        mesh_body,
        out_shape=(
            jax.ShapeDtypeStruct((3, TILES * 128), F32),
            jax.ShapeDtypeStruct((TILES, 128), F32),
        ),
        in_specs=[SMEM] * 4 + [VMEM] * 3 + [ANY] * 2 + [VMEM] * 3,
        out_specs=(VMEM, VMEM),
        scratch_shapes=[
            pltpu.SMEM((TILES + 2,), jnp.int32),
            pltpu.SMEM((TILES + 2,), jnp.int32),
            pltpu.VMEM((3, (TILES + 2) * 128), F32),
            pltpu.VMEM((TILES + 2, 8, 128), F32),
            pltpu.VMEM((CHIPS, 8, 8, 128), F32),
            pltpu.VMEM((CHIPS, 8, 8, 128), F32),
            pltpu.SemaphoreType.DMA((2,)),
        ],
        compiler_params=pltpu.CompilerParams(vmem_limit_bytes=24 * 2**20),
        name="rbf_and_flux",
    )(first, count, low, high, low, high, nodes, same, other, area, nbr, old)


def send_body(panel_ref, xyz_ref, rhs_ref, send_ref, held_ref, sems):
    parts = [slice(32 * i, 32 * i + 32) for i in range(4)]
    fetches = [pltpu.make_async_copy(panel_ref.at[p], held_ref.at[p], sems.at[i]) for i, p in enumerate(parts)]
    for fetch in fetches:
        fetch.start()
    held_ref[128:136, :] = jnp.zeros((8, ORDER), F32)
    held_ref[128:131, 0:128] = xyz_ref[...]
    held_ref[131:134, 0:128] = rhs_ref[...]
    parts.append(slice(128, 136))
    sends = [pltpu.make_async_copy(held_ref.at[p], send_ref.at[p], sems.at[4 + i]) for i, p in enumerate(parts)]
    sends[4].start()
    for fetch, send in zip(fetches, sends):
        fetch.wait()
        send.start()
    for send in sends:
        send.wait()


def pack_send(panel, xyz, rhs):
    return pl.pallas_call(
        send_body,
        out_shape=jax.ShapeDtypeStruct((136, ORDER), F32),
        in_specs=[ANY, VMEM, VMEM],
        out_specs=ANY,
        scratch_shapes=[pltpu.VMEM((136, ORDER), F32), pltpu.SemaphoreType.DMA((9,))],
        name="pack_panel",
    )(panel, xyz, rhs)


def pack_body(
    first_ref, count_ref, diag_ref, rhs_diag_ref, nodes_ref, rows_ref, head_ref, tail_ref
):
    place = lax.axis_index("vol")
    group, part = place // 4, place % 4
    for m in range(4):
        column = lax.rem(group + m, 8) * 128
        value = diag_ref[:, pl.ds(pl.multiple_of(column, 128), 128)]
        rows_ref[:, :, 128 * m : 128 * m + 128] = jnp.broadcast_to(value, (CHIPS, 32, 128))
    tall = jnp.concatenate([jnp.zeros((3, 32), F32), rhs_diag_ref[...], jnp.zeros((2, 32), F32)], axis=0)
    wide = jnp.concatenate([tall, jnp.zeros((8, 96), F32)], axis=1)
    column = jnp.concatenate([wide, jnp.zeros((120, 128), F32)], axis=0).T[0:32]
    column = column + pltpu.roll(column, 64, axis=1)
    half = lax.broadcasted_iota(jnp.int32, (32, 128), 1) // 64
    kept = jnp.where(group < 4, part // 2, 1 - part // 2)
    fifth = diag_ref[:, pl.ds(pl.multiple_of(lax.rem(group + 4, 8) * 128, 128), 128)]
    rows_ref[:, :, 512:640] = jnp.broadcast_to(jnp.where(half == kept, fifth, column), (CHIPS, 32, 128))
    row_id = lax.broadcasted_iota(jnp.int32, (8, 128), 0)
    lane = lax.broadcasted_iota(jnp.int32, (8, 128), 1)
    for edge_ref, tile in ((head_ref, 0), (tail_ref, TILES - 1)):
        first = first_ref[tile].astype(F32)
        count = count_ref[tile].astype(F32)
        lists = jnp.where(lane == 0, first, jnp.where(lane == 1, count, 0.0))
        edge_ref[...] = jnp.where(row_id == 3, lists, 0.0)
        edge_ref[0:3, :] = nodes_ref[:, 128 * tile : 128 * tile + 128]


def pack(first, count, diag, rhs_diag, nodes):
    edge = jax.ShapeDtypeStruct((8, 128), F32)
    return pl.pallas_call(
        pack_body,
        out_shape=(
            jax.ShapeDtypeStruct((CHIPS, 32, 640), F32),
            edge,
            edge,
        ),
        in_specs=[SMEM] * 2 + [VMEM] * 3,
        out_specs=(VMEM,) * 3,
        name="pack_rows",
    )(first, count, diag, rhs_diag, nodes)


def chips_to_all(copies):
    groups = [[2 * i + core for i in range(CHIPS)] for core in range(2)]
    return lax.all_to_all(copies, "vol", 0, 0, tiled=True, axis_index_groups=groups)


def other_core(blocks):
    return lax.ppermute(blocks, "vol", [(i, i ^ 1) for i in range(2 * CHIPS)])


def per_device(
    diag_block,
    rhs_diag,
    panel_block,
    rhs_panel,
    trail,
    ctrl_xyz,
    node_xyz,
    tile_blocks,
    tile_count,
    face_area,
    edge_nbr,
    old_volume,
):
    firsts = tile_blocks[:, 0]
    rows, head, tail = pack(firsts, tile_count, diag_block, rhs_diag, node_xyz)
    column_rows = lax.all_gather(pack_send(panel_block, ctrl_xyz, rhs_panel), "chol", axis=0, tiled=False)
    same_rows = chips_to_all(rows)
    other_rows = other_core(same_rows)
    size = lax.axis_size("vol")
    low = lax.ppermute(tail, "vol", [(i, i + 1) for i in range(size - 1)])
    high = lax.ppermute(head, "vol", [(i + 1, i) for i in range(size - 1)])
    other_rows, low, high = lax.optimization_barrier((other_rows, low, high))
    x, rhs_solved = solve_system(same_rows, other_rows, panel_block)
    same_ctrl = chips_to_all(control_weights(rhs_solved, column_rows))
    trail_out = apply_products(x, column_rows, trail)
    same_ctrl, trail_out = lax.optimization_barrier((same_ctrl, trail_out))
    other_ctrl = other_core(same_ctrl)
    node_disp, new_volume = update_mesh(
        firsts, tile_count, low, high, node_xyz, same_ctrl, other_ctrl, face_area, edge_nbr, old_volume.reshape(TILES, 128)
    )
    return (trail_out, node_disp, new_volume.reshape(-1))


def solution(mesh):
    return jax.shard_map(
        per_device,
        mesh=mesh,
        in_specs=(
            P("vol", None),
            P(None, "vol"),
            P(("chol", "vol"), None),
            P(None, ("chol", "vol")),
            P(("chol", "vol"), None),
            P(None, ("chol", "vol")),
            P(None, ("chol", "vol")),
            P(("chol", "vol"), None),
            P(("chol", "vol")),
            P(None, None, ("chol", "vol")),
            P(None, ("chol", "vol")),
            P(("chol", "vol")),
        ),
        out_specs=(P(("chol", "vol"), None), P(None, ("chol", "vol")), P(("chol", "vol"))),
        check_vma=False,
    )
```

```python
import jax
import jax.numpy as jnp
from jax import lax
from jax.experimental import pallas as pl
from jax.experimental.pallas import tpu as pltpu
from jax.sharding import PartitionSpec as P

F32 = jnp.float32
BF16 = jnp.bfloat16
NN = (((1,), (0,)), ((), ()))
NT = (((1,), (1,)), ((), ()))
WIDE = 256
STEPS = 4
CHIPS = 16
ORDER = 1024
SIDE = 256
VMEM = pl.BlockSpec(memory_space=pltpu.VMEM)
SMEM = pl.BlockSpec(memory_space=pltpu.SMEM)
ANY = pl.BlockSpec(memory_space=pl.ANY)


def split(value):
    high = value.astype(BF16)
    return high, (value - high.astype(F32)).astype(BF16)


def raw_dot(left, right, dims=NN):
    return lax.dot_general(left, right, dims, preferred_element_type=F32)


def product(left, right, dims=NN):
    left_high, left_low = left
    right_high, right_low = right
    return (
        raw_dot(left_high, right_low, dims) + raw_dot(left_low, right_high, dims)
    ) + raw_dot(left_high, right_high, dims)


def inverse(block):
    size = block.shape[0]
    row_id = lax.broadcasted_iota(jnp.int32, (size, size), 0)
    col_id = lax.broadcasted_iota(jnp.int32, (size, size), 1)
    on_diag = row_id == col_id
    only_diag = jnp.where(on_diag, block, 0.0)
    diag_col = jnp.sum(only_diag, axis=1, keepdims=True)
    diag_row = jnp.sum(only_diag, axis=0, keepdims=True)
    power = jnp.where(on_diag, 0.0, -block / diag_col)
    total = jnp.where(on_diag, 1.0, power)
    parts = split(power)
    power = product(parts, parts)

    def stage(power, total):
        parts = split(power)
        return product(parts, parts), total + product(split(total), parts)

    for _ in range(4):
        power, total = stage(power, total)
    total = total + product(split(total), split(power))

    def left_over(power):
        return size * jnp.max(jnp.abs(power)) ** 2

    def unfinished(state):
        return (state[2] > 1e-7) & (state[3] < 40)

    def more(state):
        power, total, _, count = state
        parts = split(power)
        power = product(parts, parts)
        total = total + product(split(total), split(power))
        return power, total, left_over(power), count + 1

    total = lax.while_loop(unfinished, more, (power, total, left_over(power), 0))[1]
    return total / diag_row


def factor_body(same_ref, other_ref, panel_ref, out_ref, rhs_ref, rows_ref, m_ref, vh_ref, vl_ref):
    full = ORDER + SIDE
    core = lax.axis_index("vol") % 2
    for i in range(16):
        rows_ref[pl.ds(pl.multiple_of(64 * i + 32 * core, 32), 32), :] = same_ref[i]
        rows_ref[pl.ds(pl.multiple_of(64 * i + 32 * (1 - core), 32), 32), :] = other_ref[i]
    half_row = lax.broadcasted_iota(jnp.int32, (128, 128), 0) // 64
    half_col = lax.broadcasted_iota(jnp.int32, (128, 128), 1) // 64
    lane = lax.broadcasted_iota(jnp.int32, (128, 128), 1)
    def rows_of(g, m):
        return rows_ref[128 * g : 128 * g + 128, 128 * m : 128 * m + 128]
    for g in range(8):
        for h in range(g, 8):
            m = h - g
            if m < 4:
                block = rows_of(g, m)
            elif m == 4:
                block = jnp.where(half_row == half_col, rows_of(g, 4), rows_of(h, 4).T)
            else:
                block = rows_of(h, 8 - m).T
            m_ref[128 * g : 128 * g + 128, 128 * h : 128 * h + 128] = block
            if m == 1 and g % 2 == 0:
                m_ref[128 * h : 128 * h + 128, 128 * g : 128 * g + 128] = block.T
        m_ref[128 * g : 128 * g + 128, ORDER : ORDER + 128] = panel_ref[:, 128 * g : 128 * g + 128].T
        spare = rows_of(g, 4)
        turned = pltpu.roll(spare, 64, axis=1)
        first_half = (half_row == 1) if g < 4 else (half_row == 0)
        right = jnp.where(first_half, spare, turned)
        m_ref[128 * g : 128 * g + 128, ORDER + 128 : full] = jnp.where((lane >= 3) & (lane < 6), right, 0.0)
    for k in range(STEPS):
        here = slice(WIDE * k, WIDE * (k + 1))
        later = WIDE * (k + 1)
        inv = split(inverse(m_ref[here, here]))
        values = product(inv, split(m_ref[here, later:full]))
        if k < STEPS - 1:
            high, low = split(values)
            vh_ref[here, later:full] = high
            vl_ref[here, later:full] = low
            for i in range(k + 1, STEPS):
                there = slice(WIDE * i, WIDE * (i + 1))
                left = split(m_ref[here, there].T)
                start = WIDE * (i - k - 1)
                m_ref[there, WIDE * i : full] -= product(left, (high[:, start:], low[:, start:]))
        else:
            out_ref[here, :] = values
    for k in range(STEPS - 2, -1, -1):
        here = slice(WIDE * k, WIDE * (k + 1))
        later = WIDE * (k + 1)
        own = vh_ref[here, ORDER:full].astype(F32) + vl_ref[here, ORDER:full].astype(F32)
        left = (vh_ref[here, later:ORDER], vl_ref[here, later:ORDER])
        out_ref[here, :] = own - product(left, split(out_ref[later:ORDER, :]))
    for g in range(8):
        here = slice(128 * g, 128 * g + 128)
        high, low = split(out_ref[here, 128:256].T[0:8])
        rhs_ref[:, here] = jnp.concatenate([high, low], axis=0)


def solve_system(same, other, panel):
    full = ORDER + SIDE
    return pl.pallas_call(
        factor_body,
        out_shape=(jax.ShapeDtypeStruct((ORDER, SIDE), F32), jax.ShapeDtypeStruct((16, ORDER), BF16)),
        in_specs=[VMEM] * 3,
        out_specs=(VMEM, VMEM),
        scratch_shapes=[
            pltpu.VMEM((ORDER, 640), F32),
            pltpu.VMEM((ORDER, full), F32),
            pltpu.VMEM((ORDER, full), BF16),
            pltpu.VMEM((ORDER, full), BF16),
        ],
        compiler_params=pltpu.CompilerParams(vmem_limit_bytes=56 * 2**20),
        name="block_elimination",
    )(same, other, panel)


SLOTS = 8
TILES = 64
RADIUS = 1.25
PHI_SCALE = 4.0 * 0.8**5
UNROLL = 11
COMMON = 5
MARGIN = 1e-3


def weights_body(rhs_ref, rows_ref, ctrl_ref):
    for c in range(4):
        high, low = split(rows_ref[c, 0:128, :])
        by_high = raw_dot(rhs_ref[...], high, NT)
        by_low = raw_dot(rhs_ref[...], low, NT)
        ctrl = rows_ref[c, 128:136, 0:128] - (by_low[0:8] + by_high[8:16] + by_high[0:8])
        ctrl_ref[:, c] = jnp.broadcast_to(ctrl, (CHIPS, 8, 128))


def control_weights(rhs, rows):
    return pl.pallas_call(
        weights_body,
        out_shape=jax.ShapeDtypeStruct((CHIPS, 8, 8, 128), F32),
        grid=(2,),
        in_specs=[
            pl.BlockSpec((16, ORDER), lambda c: (0, 0)),
            pl.BlockSpec((4, 136, ORDER), lambda c: (c, 0, 0)),
        ],
        out_specs=pl.BlockSpec((CHIPS, 4, 8, 128), lambda c: (0, c, 0, 0)),
        compiler_params=pltpu.CompilerParams(vmem_limit_bytes=60 * 2**20),
        name="control_weights",
    )(rhs, rows)


def products_body(x_ref, rows_ref, trail_ref, out_ref, high_ref, low_ref):
    @pl.when(pl.program_id(0) == 0)
    def _():
        high_ref[...], low_ref[...] = split(x_ref[...])

    sums = product(split(rows_ref[0, 0:128, :]), (high_ref[...], low_ref[...]))
    out_ref[...] = trail_ref[...] - sums.T


def apply_products(x, rows, trail):
    return pl.pallas_call(
        products_body,
        out_shape=jax.ShapeDtypeStruct((128, ORDER), F32),
        grid=(8,),
        in_specs=[
            pl.BlockSpec((ORDER, 128), lambda c: (0, 0)),
            pl.BlockSpec((1, 136, ORDER), lambda c: (c, 0, 0)),
            pl.BlockSpec((128, 128), lambda c: (0, c)),
        ],
        out_specs=pl.BlockSpec((128, 128), lambda c: (0, c)),
        scratch_shapes=[pltpu.VMEM((ORDER, 128), BF16)] * 2,
        compiler_params=pltpu.CompilerParams(vmem_limit_bytes=60 * 2**20),
        cost_estimate=pl.CostEstimate(flops=3 * 2 * 128 * 1024 * 1024, bytes_accessed=6 * 2**20, transcendentals=0),
        name="trail_update",
    )(x, rows, trail)


def order_body(nodes_ref, low_ref, high_ref, sorted_ref, rank_ref, start_ref, stop_ref):
    down = lax.broadcasted_iota(jnp.int32, (128, 128), 0)
    along = lax.broadcasted_iota(jnp.int32, (128, 128), 1)

    def order_tile(t, xyz):
        row = jnp.broadcast_to(xyz[0:1], (128, 128))
        column = row.T
        before = (column < row) | ((column == row) & (down < along))
        rank = jnp.sum(before.astype(F32), axis=0, keepdims=True)
        rank_column = jnp.broadcast_to(rank, (128, 128)).T
        order = jnp.sum(jnp.where(rank_column == along.astype(F32), down.astype(F32), 0.0), axis=0, keepdims=True)
        order = jnp.broadcast_to(order.astype(jnp.int32), (8, 128))
        full = jnp.concatenate([xyz, jnp.zeros((5, 128), F32)], axis=0)
        full = jnp.take_along_axis(full, order, axis=1, mode="promise_in_bounds")
        sorted_ref[t] = full
        rank_ref[t] = jnp.broadcast_to(rank.astype(jnp.int32), (8, 128))
        start_ref[pl.ds(t, 1), :] = jnp.floor(full[0:1] - (RADIUS + MARGIN)).astype(jnp.int32)
        stop_ref[pl.ds(t, 1), :] = jnp.floor(full[0:1] + (RADIUS + MARGIN)).astype(jnp.int32)

    order_tile(0, low_ref[0:3])
    order_tile(TILES + 1, high_ref[0:3])

    def several(i, carry):
        for u in range(16):
            t = 16 * i + u
            order_tile(t + 1, nodes_ref[:, pl.ds(pl.multiple_of(t * 128, 128), 128)])
        return carry

    lax.fori_loop(0, TILES // 16, several, 0)


def order_nodes(nodes, low, high):
    ids = jax.ShapeDtypeStruct((TILES + 2, 128), jnp.int32)
    return pl.pallas_call(
        order_body,
        out_shape=(
            jax.ShapeDtypeStruct((TILES + 2, 8, 128), F32),
            jax.ShapeDtypeStruct((TILES + 2, 8, 128), jnp.int32),
            ids,
            ids,
        ),
        in_specs=[VMEM] * 3,
        out_specs=(VMEM,) * 4,
        cost_estimate=pl.CostEstimate(flops=20_000_000, bytes_accessed=2**20, transcendentals=0),
        name="node_order",
    )(nodes, low, high)


def phi_of(dist_sq):
    dist = dist_sq * lax.rsqrt(jnp.maximum(dist_sq, 1e-30))
    remain = jnp.maximum(RADIUS - dist, 0.0)
    remain_sq = remain * remain
    return remain_sq * remain_sq * (RADIUS * RADIUS - remain)


def group_phi(spread, ctrl_ref, blocks):
    dist_sq = None
    for a in range(3):
        differ = jnp.concatenate(
            [spread[a][16 * g : 16 * g + 16] - ctrl_ref[blocks[g], a : a + 1, :] for g in range(8)], axis=0
        )
        dist_sq = differ * differ if a == 0 else dist_sq + differ * differ
    return split(phi_of(dist_sq))


def group_sums(weight, high, low, rank):
    weight = weight.astype(BF16)
    both = raw_dot(weight, low, NT) + raw_dot(weight, high, NT)
    group_of = lax.broadcasted_iota(jnp.int32, (8, 128), 1) // 16
    total = jnp.zeros((8, 128), F32)
    for g in range(8):
        total = jnp.where(group_of == g, both[8 * g : 8 * g + 8], total)
    total = (total + pltpu.roll(total, 3, axis=0)) * PHI_SCALE
    return jnp.take_along_axis(total, rank, axis=1, mode="promise_in_bounds")


def node_columns(sorted_ref, t):
    return [jnp.broadcast_to(sorted_ref[t, a : a + 1, :], (128, 128)).T for a in range(3)]


def group_starts(t, first, start_ref):
    return [jnp.clip(start_ref[t, 16 * g] - first, 0, SLOTS - 1) for g in range(8)]


def tile_sum(t, u, first, count, start_ref, stop_ref, sorted_ref, rank_ref, ctrl_ref, weight_ref):
    row_id = lax.broadcasted_iota(jnp.int32, (8, 128), 0)
    for s in range(SLOTS):
        live = s < count
        ctrl = ctrl_ref[jnp.where(live, first + s, first)]
        ctrl = jnp.where(live, ctrl, 0.0)
        high = ctrl.astype(BF16).astype(F32)
        low = pltpu.roll(ctrl - high, 5, axis=0)
        weight_ref[u, :, 128 * s : 128 * s + 128] = jnp.where(row_id < 3, low, jnp.where(row_id < 6, high, 0.0))
    starts = group_starts(t, first, start_ref)
    most = jnp.int32(0)
    for g in range(8):
        most = jnp.maximum(most, jnp.clip(stop_ref[t, 16 * g + 15] - first, 0, count - 1) - starts[g] + 1)
    spread = node_columns(sorted_ref, t)
    parts = [
        group_phi(spread, ctrl_ref, [jnp.minimum(first + starts[g] + j, 255) for g in range(8)]) for j in range(COMMON)
    ]
    weight = jnp.concatenate(
        [weight_ref[u, :, pl.ds(pl.multiple_of(starts[g] * 128, 128), COMMON * 128)] for g in range(8)], axis=0
    )
    high = jnp.concatenate([part[0] for part in parts], axis=1)
    low = jnp.concatenate([part[1] for part in parts], axis=1)
    return group_sums(weight, high, low, rank_ref[t]), most


def tile_rest(t, u, first, most, start_ref, sorted_ref, rank_ref, ctrl_ref, weight_ref, d_ref):
    starts = group_starts(t, first, start_ref)

    def step(j, carry):
        spread = node_columns(sorted_ref, t)
        high, low = group_phi(spread, ctrl_ref, [jnp.minimum(first + starts[g] + j, 255) for g in range(8)])
        weight = jnp.concatenate(
            [
                weight_ref[u, :, pl.ds(pl.multiple_of(jnp.minimum(starts[g] + j, SLOTS) * 128, 128), 128)]
                for g in range(8)
            ],
            axis=0,
        )
        d_ref[t] = d_ref[t] + group_sums(weight, high, low, rank_ref[t])
        return carry

    lax.fori_loop(COMMON, most, step, 0)


def mesh_body(
    tile_first_ref,
    tile_count_ref,
    low_list_ref,
    high_list_ref,
    start_ref,
    stop_ref,
    sorted_ref,
    rank_ref,
    same_any,
    other_any,
    area_ref,
    nbr_ref,
    old_ref,
    disp_ref,
    volume_ref,
    first_ref,
    count_ref,
    most_ref,
    d_ref,
    same_ref,
    other_ref,
    ctrl_ref,
    weight_ref,
    sems,
):
    copies = [
        pltpu.make_async_copy(same_any, same_ref, sems.at[0]),
        pltpu.make_async_copy(other_any, other_ref, sems.at[1]),
    ]
    for copy in copies:
        copy.start()

    def lists(t, carry):
        first_ref[t + 1] = tile_first_ref[0, t]
        count_ref[t + 1] = tile_count_ref[t]
        return carry

    lax.fori_loop(0, TILES, lists, 0)
    for t, list_ref in ((0, low_list_ref), (TILES + 1, high_list_ref)):
        first_ref[t] = list_ref[3, 0].astype(jnp.int32)
        count_ref[t] = list_ref[3, 1].astype(jnp.int32)
    weight_ref[:, :, SLOTS * 128 :] = jnp.zeros((UNROLL, 8, COMMON * 128), F32)

    def flux_tile(t):
        here = pl.ds(pl.multiple_of(t * 128, 128), 128)
        index = nbr_ref[:, here] - t * 128
        which = index // 128
        lane = index - which * 128
        low, own, high = d_ref[t], d_ref[t + 1], d_ref[t + 2]
        disp_ref[:, here] = own[3:6]
        flux = jnp.zeros((6, 128), F32)
        for a in range(3):
            near = [
                jnp.take_along_axis(
                    jnp.broadcast_to(v[3 + a : 4 + a], (6, 128)), lane, axis=1, mode="promise_in_bounds"
                )
                for v in (low, own, high)
            ]
            across = jnp.where(which == 0, near[0], jnp.where(which == 1, near[1], near[2]))
            flux = flux + area_ref[a, :, here] * (own[3 + a : 4 + a] + across)
        volume_ref[pl.ds(t, 1), :] = old_ref[pl.ds(t, 1), :] + 0.5 * jnp.sum(flux, axis=0, keepdims=True)

    def sums(i, carry):
        for u in range(UNROLL):
            flux_tile(jnp.maximum((i - 1) * UNROLL + u - 2, 0))
        most = jnp.int32(0)
        for u in range(UNROLL):
            t = i * UNROLL + u
            d_ref[t], need = tile_sum(
                t, u, first_ref[t], count_ref[t], start_ref, stop_ref, sorted_ref, rank_ref, ctrl_ref, weight_ref
            )
            most_ref[u] = need
            most = jnp.maximum(most, need)

        @pl.when(most > COMMON)
        def _():
            def rest(u, carry):
                t = i * UNROLL + u
                tile_rest(
                    t, u, first_ref[t], most_ref[u], start_ref, sorted_ref, rank_ref, ctrl_ref, weight_ref, d_ref
                )
                return carry

            lax.fori_loop(0, UNROLL, rest, 0)

        return carry

    d_ref[0:3] = jnp.zeros((3, 8, 128), F32)
    for copy in copies:
        copy.wait()
    core = lax.axis_index("vol") % 2
    for chip in range(CHIPS):
        for rank in range(8):
            ctrl_ref[32 * rank + 2 * chip + core] = same_ref[chip, rank]
            ctrl_ref[32 * rank + 2 * chip + 1 - core] = other_ref[chip, rank]
    lax.fori_loop(0, (TILES + 2) // UNROLL, sums, 0)
    for u in range(UNROLL):
        flux_tile(TILES - UNROLL + u)


def update_mesh(first, count, low, high, start, stop, nodes, rank, same, other, area, nbr, old):
    return pl.pallas_call(
        mesh_body,
        out_shape=(
            jax.ShapeDtypeStruct((3, TILES * 128), F32),
            jax.ShapeDtypeStruct((TILES, 128), F32),
        ),
        in_specs=[SMEM] * 6 + [VMEM] * 2 + [ANY] * 2 + [VMEM] * 3,
        out_specs=(VMEM, VMEM),
        scratch_shapes=[
            pltpu.SMEM((TILES + 2,), jnp.int32),
            pltpu.SMEM((TILES + 2,), jnp.int32),
            pltpu.SMEM((UNROLL,), jnp.int32),
            pltpu.VMEM((TILES + 2, 8, 128), F32),
            pltpu.VMEM((CHIPS, 8, 8, 128), F32),
            pltpu.VMEM((CHIPS, 8, 8, 128), F32),
            pltpu.VMEM((256, 8, 128), F32),
            pltpu.VMEM((UNROLL, 8, (SLOTS + COMMON) * 128), F32),
            pltpu.SemaphoreType.DMA((2,)),
        ],
        compiler_params=pltpu.CompilerParams(vmem_limit_bytes=32 * 2**20),
        name="rbf_and_flux",
    )(first, count, low, high, start, stop, nodes, rank, same, other, area, nbr, old)


def send_body(panel_ref, xyz_ref, rhs_ref, send_ref, held_ref, sems):
    parts = [slice(32 * i, 32 * i + 32) for i in range(4)]
    fetches = [pltpu.make_async_copy(panel_ref.at[p], held_ref.at[p], sems.at[i]) for i, p in enumerate(parts)]
    for fetch in fetches:
        fetch.start()
    held_ref[128:136, :] = jnp.zeros((8, ORDER), F32)
    held_ref[128:131, 0:128] = xyz_ref[...]
    held_ref[131:134, 0:128] = rhs_ref[...]
    parts.append(slice(128, 136))
    sends = [pltpu.make_async_copy(held_ref.at[p], send_ref.at[p], sems.at[4 + i]) for i, p in enumerate(parts)]
    sends[4].start()
    for fetch, send in zip(fetches, sends):
        fetch.wait()
        send.start()
    for send in sends:
        send.wait()


def pack_send(panel, xyz, rhs):
    return pl.pallas_call(
        send_body,
        out_shape=jax.ShapeDtypeStruct((136, ORDER), F32),
        in_specs=[ANY, VMEM, VMEM],
        out_specs=ANY,
        scratch_shapes=[pltpu.VMEM((136, ORDER), F32), pltpu.SemaphoreType.DMA((9,))],
        name="pack_panel",
    )(panel, xyz, rhs)


def pack_body(
    first_ref, count_ref, diag_ref, rhs_diag_ref, nodes_ref, rows_ref, head_ref, tail_ref
):
    place = lax.axis_index("vol")
    group, part = place // 4, place % 4
    for m in range(4):
        column = lax.rem(group + m, 8) * 128
        value = diag_ref[:, pl.ds(pl.multiple_of(column, 128), 128)]
        rows_ref[:, :, 128 * m : 128 * m + 128] = jnp.broadcast_to(value, (CHIPS, 32, 128))
    tall = jnp.concatenate([jnp.zeros((3, 32), F32), rhs_diag_ref[...], jnp.zeros((2, 32), F32)], axis=0)
    wide = jnp.concatenate([tall, jnp.zeros((8, 96), F32)], axis=1)
    column = jnp.concatenate([wide, jnp.zeros((120, 128), F32)], axis=0).T[0:32]
    column = column + pltpu.roll(column, 64, axis=1)
    half = lax.broadcasted_iota(jnp.int32, (32, 128), 1) // 64
    kept = jnp.where(group < 4, part // 2, 1 - part // 2)
    fifth = diag_ref[:, pl.ds(pl.multiple_of(lax.rem(group + 4, 8) * 128, 128), 128)]
    rows_ref[:, :, 512:640] = jnp.broadcast_to(jnp.where(half == kept, fifth, column), (CHIPS, 32, 128))
    row_id = lax.broadcasted_iota(jnp.int32, (8, 128), 0)
    lane = lax.broadcasted_iota(jnp.int32, (8, 128), 1)
    for edge_ref, tile in ((head_ref, 0), (tail_ref, TILES - 1)):
        first = first_ref[0, tile].astype(F32)
        count = count_ref[tile].astype(F32)
        lists = jnp.where(lane == 0, first, jnp.where(lane == 1, count, 0.0))
        edge_ref[...] = jnp.where(row_id == 3, lists, 0.0)
        edge_ref[0:3, :] = nodes_ref[:, 128 * tile : 128 * tile + 128]


def pack(first, count, diag, rhs_diag, nodes):
    edge = jax.ShapeDtypeStruct((8, 128), F32)
    return pl.pallas_call(
        pack_body,
        out_shape=(
            jax.ShapeDtypeStruct((CHIPS, 32, 640), F32),
            edge,
            edge,
        ),
        in_specs=[SMEM] * 2 + [VMEM] * 3,
        out_specs=(VMEM,) * 3,
        name="pack_rows",
    )(first, count, diag, rhs_diag, nodes)


def chips_to_all(copies):
    groups = [[2 * i + core for i in range(CHIPS)] for core in range(2)]
    return lax.all_to_all(copies, "vol", 0, 0, tiled=True, axis_index_groups=groups)


def other_core(blocks):
    return lax.ppermute(blocks, "vol", [(i, i ^ 1) for i in range(2 * CHIPS)])


def per_device(
    diag_block,
    rhs_diag,
    panel_block,
    rhs_panel,
    trail,
    ctrl_xyz,
    node_xyz,
    tile_blocks,
    tile_count,
    face_area,
    edge_nbr,
    old_volume,
):
    firsts = tile_blocks.T
    rows, head, tail = pack(firsts, tile_count, diag_block, rhs_diag, node_xyz)
    column_rows = lax.all_gather(pack_send(panel_block, ctrl_xyz, rhs_panel), "chol", axis=0, tiled=False)
    same_rows = chips_to_all(rows)
    other_rows = other_core(same_rows)
    size = lax.axis_size("vol")
    low = lax.ppermute(tail, "vol", [(i, i + 1) for i in range(size - 1)])
    high = lax.ppermute(head, "vol", [(i + 1, i) for i in range(size - 1)])
    other_rows, low, high = lax.optimization_barrier((other_rows, low, high))
    in_order, ranks, start, stop = order_nodes(node_xyz, low, high)
    x, rhs_solved = solve_system(same_rows, other_rows, panel_block)
    rhs_solved, in_order, ranks, start, stop = lax.optimization_barrier((rhs_solved, in_order, ranks, start, stop))
    same_ctrl = chips_to_all(control_weights(rhs_solved, column_rows))
    trail_out = apply_products(x, column_rows, trail)
    same_ctrl, trail_out = lax.optimization_barrier((same_ctrl, trail_out))
    other_ctrl = other_core(same_ctrl)
    node_disp, new_volume = update_mesh(
        firsts, tile_count, low, high, start, stop, in_order, ranks, same_ctrl, other_ctrl, face_area, edge_nbr, old_volume.reshape(TILES, 128)
    )
    return (trail_out, node_disp, new_volume.reshape(-1))


def solution(mesh):
    return jax.shard_map(
        per_device,
        mesh=mesh,
        in_specs=(
            P("vol", None),
            P(None, "vol"),
            P(("chol", "vol"), None),
            P(None, ("chol", "vol")),
            P(("chol", "vol"), None),
            P(None, ("chol", "vol")),
            P(None, ("chol", "vol")),
            P(("chol", "vol"), None),
            P(("chol", "vol")),
            P(None, None, ("chol", "vol")),
            P(None, ("chol", "vol")),
            P(("chol", "vol")),
        ),
        out_specs=(P(("chol", "vol"), None), P(None, ("chol", "vol")), P(("chol", "vol"))),
        check_vma=False,
    )
```
